32 devices in a mesh: seq: 16 (over z, y, core), ch: 2 (over x).
Axes of the slice: x: 2, y: 2, z: 4, core: 2. Of those that a mesh axis runs over, the one named last changes fastest.
Arguments:
- q_saved: bfloat16 [4096, 4096], P('seq', 'ch'), may hold values from -6 to 6
- k_saved: bfloat16 [4096, 4096], P('seq', 'ch'), may hold values from -6 to 6
- v_saved: bfloat16 [4096, 4096], P('seq', 'ch'), may hold values from -6 to 6
- grad_out: bfloat16 [4096, 4096], P('seq', 'ch'), may hold values from -6 to 6
- residue: float32 [4096, 64], P(('ch', 'seq')), may hold values from -0.15 to 0.15
- rate: float32 [4, 64], replicated, may hold values from 0.5 to 500
- freq_mix: float32 [4, 64, 16], replicated, may hold values from -4 to 4
Outputs:
- grad_q: bfloat16 [4096, 4096], P('seq', 'ch')
- grad_k: bfloat16 [4096, 4096], P('seq', 'ch')
- grad_v: bfloat16 [4096, 4096], P('seq', 'ch')
- grad_residue: float32 [4096, 64], P(('ch', 'seq'))
- grad_rate: float32 [4, 64], replicated
- grad_mix: float32 [4, 64, 16], replicated
The draws below stay inside these ranges and needn't reach their ends.
All inputs are finite; a program needn't handle non-finite values.
Results may differ from the reference program's by a relative error of at most 0.0089.
Values may be sent and summed in bfloat16 or wider, within the bound.
A program may use at most 128 MiB of HBM per device.

```python
import math
import jax
import jax.numpy as jnp
import numpy as np
from jax import lax

C = 4096
MODES = 64
FEATS = 16
GROUPS = 4
TOKENS = 4096


def level_of(rng, dims, split, smallest, high):
    loudness, own = 1.0, jax.random.fold_in(rng, 6)
    for position, parts in split:
        heights = jnp.exp(jax.random.uniform(jax.random.fold_in(own, position), (parts,), jnp.float32, smallest / len(split), high / len(split)))
        loudness = loudness * jnp.repeat(heights, dims[position] // parts).reshape([-1 if axis == position else 1 for axis in range(len(dims))])
    return loudness


def normal_values(rng, extent, spread, bound, shards=(), kind=jnp.bfloat16):
    values = jax.random.normal(rng, extent, jnp.float32) * spread
    if len(shards) > 0:
        values = level_of(rng, extent, shards, -0.22, 0.18) * values
    return jnp.clip(values, min=-bound, max=bound).astype(kind)


def setup_inputs(seed: int = 0) -> dict:
    seeds = jax.random.split(jax.random.key(seed), 8)
    return {
        "q_saved": normal_values(seeds[0], (TOKENS, C), 1.0, 6.0, ((0, 16), (1, 2))),
        "k_saved": normal_values(seeds[1], (TOKENS, C), 1.0, 6.0, ((0, 16), (1, 2))),
        "v_saved": normal_values(seeds[2], (TOKENS, C), 1.0, 6.0, ((0, 16), (1, 2))),
        "grad_out": normal_values(seeds[3], (TOKENS, C), 1.0, 6.0, ((0, 16), (1, 2))),
        "residue": normal_values(seeds[4], (C, MODES), 0.025, 0.15, ((0, 32),), jnp.float32),
        "rate": jnp.clip(jnp.exp(jax.random.uniform(seeds[5], (GROUPS, MODES), jnp.float32, math.log(0.5), math.log(500.0))), 0.5, 500.0),
        "freq_mix": normal_values(seeds[6], (GROUPS, MODES, FEATS), 1.0, 4.0, (), jnp.float32),
    }


HIGH = lax.Precision.HIGHEST


def split_length(padded):
    best = 1
    candidate = 1
    while candidate * candidate <= padded:
        if padded % candidate == 0:
            best = candidate
        candidate += 1
    return padded // best, best


def angle_table(rows_count, cols_count, period):
    row_index = jnp.arange(rows_count, dtype=jnp.int32)[:, None]
    col_index = jnp.arange(cols_count, dtype=jnp.int32)[None, :]
    phase = ((row_index * col_index) % period).astype(jnp.float32) * (2.0 * math.pi / period)
    return jnp.cos(phase), jnp.sin(phase)


def make_tables(length):
    padded = 2 * length
    outer, inner = split_length(padded)
    outer_cos, outer_sin = angle_table(outer, outer // 2, outer)
    twid_cos, twid_sin = angle_table(outer, inner, padded)
    inner_cos, inner_sin = angle_table(inner, inner, inner)
    return (outer, inner, outer_cos.astype(jnp.bfloat16), outer_sin.astype(jnp.bfloat16), twid_cos, twid_sin,
            inner_cos.astype(jnp.bfloat16), inner_sin.astype(jnp.bfloat16))


def position_features(length, feat_count):
    freqs = jnp.array(np.array([3 ** j for j in range(feat_count // 2)]), dtype=jnp.int32)
    steps = jnp.arange(length, dtype=jnp.int32)
    phase = ((freqs[:, None] * steps[None, :]) % length).astype(jnp.float32) * (2.0 * math.pi / length)
    return jnp.stack([jnp.cos(phase), jnp.sin(phase)], axis=1).reshape(feat_count, length)


def forward_dft(signal, tables):
    outer, inner, outer_cos, outer_sin, twid_cos, twid_sin, inner_cos, inner_sin = tables
    blocks = signal.reshape(signal.shape[0], outer // 2, inner)
    part_re = jnp.einsum("kn,cnb->ckb", outer_cos, blocks, preferred_element_type=jnp.float32)
    part_im = -jnp.einsum("kn,cnb->ckb", outer_sin, blocks, preferred_element_type=jnp.float32)
    turn_re = (part_re * twid_cos + part_im * twid_sin).astype(jnp.bfloat16)
    turn_im = (part_im * twid_cos - part_re * twid_sin).astype(jnp.bfloat16)
    spec_re = jnp.einsum("ckn,nm->ckm", turn_re, inner_cos, preferred_element_type=jnp.float32) + jnp.einsum("ckn,nm->ckm", turn_im, inner_sin, preferred_element_type=jnp.float32)
    spec_im = jnp.einsum("ckn,nm->ckm", turn_im, inner_cos, preferred_element_type=jnp.float32) - jnp.einsum("ckn,nm->ckm", turn_re, inner_sin, preferred_element_type=jnp.float32)
    return spec_re, spec_im


def inverse_dft(spec_re, spec_im, tables):
    outer, inner, outer_cos, outer_sin, twid_cos, twid_sin, inner_cos, inner_sin = tables
    part_re = jnp.einsum("ckm,mn->ckn", spec_re, inner_cos, preferred_element_type=jnp.float32) - jnp.einsum("ckm,mn->ckn", spec_im, inner_sin, preferred_element_type=jnp.float32)
    part_im = jnp.einsum("ckm,mn->ckn", spec_re, inner_sin, preferred_element_type=jnp.float32) + jnp.einsum("ckm,mn->ckn", spec_im, inner_cos, preferred_element_type=jnp.float32)
    turn_re = (part_re * twid_cos - part_im * twid_sin).astype(jnp.bfloat16)
    turn_im = (part_re * twid_sin + part_im * twid_cos).astype(jnp.bfloat16)
    values = jnp.einsum("kn,ckb->cnb", outer_cos, turn_re, preferred_element_type=jnp.float32) - jnp.einsum("kn,ckb->cnb", outer_sin, turn_im, preferred_element_type=jnp.float32)
    return values.reshape(values.shape[0], (outer // 2) * inner) / (outer * inner)


def spectral_products(first, second, conjugate):
    if conjugate:
        real_part = first[0] * second[0] + first[1] * second[1]
        imag_part = first[0] * second[1] - first[1] * second[0]
    else:
        real_part = first[0] * second[0] - first[1] * second[1]
        imag_part = first[0] * second[1] + first[1] * second[0]
    return real_part.astype(jnp.bfloat16), imag_part.astype(jnp.bfloat16)


def channel_work(gated_rows, grad_rows, filter_rows, tables):
    spec_u = forward_dft(gated_rows, tables)
    spec_z = forward_dft(grad_rows, tables)
    spec_h = forward_dft(filter_rows, tables)
    conv = inverse_dft(*spectral_products(spec_h, spec_u, False), tables)
    corr = inverse_dft(*spectral_products(spec_h, spec_z, True), tables)
    dfilter = inverse_dft(*spectral_products(spec_u, spec_z, True), tables)
    return conv.astype(jnp.bfloat16), corr.astype(jnp.bfloat16), dfilter


def reference(q_saved, k_saved, v_saved, grad_out, residue, rate, freq_mix):
    length = TOKENS
    per_group = C // GROUPS
    gated = (k_saved.astype(jnp.float32) * v_saved.astype(jnp.float32)).astype(jnp.bfloat16)
    gated_grad = (grad_out.astype(jnp.float32) * q_saved.astype(jnp.float32)).astype(jnp.bfloat16)
    times = jnp.arange(length, dtype=jnp.float32) / length
    feats = position_features(length, FEATS)
    pre = jnp.einsum("gmk,kl->gml", freq_mix, feats, precision=HIGH)
    window = jnp.exp(-rate[:, :, None] * times[None, None, :])
    basis = jnp.sin(pre) * window
    res_groups = residue.reshape(GROUPS, per_group, MODES)
    filt = jnp.einsum("gcm,gml->gcl", res_groups, basis, precision=HIGH).reshape(C, length).astype(jnp.bfloat16)
    tables = make_tables(length)
    block = min(C, 256)
    count = C // block
    gated_t = gated.T.reshape(count, block, length)
    grad_t = gated_grad.T.reshape(count, block, length)
    filt_b = filt.reshape(count, block, length)

    def one_block(items):
        return channel_work(items[0], items[1], items[2], tables)

    conv, corr, dfilter = lax.map(one_block, (gated_t, grad_t, filt_b))
    conv_b = conv.reshape(C, length).T
    corr_b = corr.reshape(C, length).T
    dfilter = dfilter.reshape(C, length)
    grad_q = (grad_out.astype(jnp.float32) * conv_b.astype(jnp.float32)).astype(jnp.bfloat16)
    grad_k = (corr_b.astype(jnp.float32) * v_saved.astype(jnp.float32)).astype(jnp.bfloat16)
    grad_v = (corr_b.astype(jnp.float32) * k_saved.astype(jnp.float32)).astype(jnp.bfloat16)
    dfilt_groups = dfilter.reshape(GROUPS, per_group, length)
    grad_residue = jnp.einsum("gcl,gml->gcm", dfilt_groups, basis, precision=HIGH).reshape(C, MODES) / length
    mixed = jnp.einsum("gcl,gcm->gml", dfilt_groups, res_groups, precision=HIGH)
    grad_rate = -jnp.sum(mixed * times[None, None, :] * basis, axis=2) / length
    slope = mixed * window * jnp.cos(pre)
    grad_mix = jnp.einsum("gml,kl->gmk", slope, feats, precision=HIGH) / length
    return grad_q, grad_k, grad_v, grad_residue, grad_rate, grad_mix
```

```python
import functools
import math

import jax
import jax.numpy as jnp
import numpy as np
from jax import lax
from jax.experimental import pallas as pl
from jax.experimental.pallas import tpu as pltpu
from jax.sharding import PartitionSpec as P

C = 4096
FEATS = 16
GROUPS = 4
LANES = 128


HIGH = lax.Precision.HIGHEST


def split_length(padded):
    best = 1
    candidate = 1
    while candidate * candidate <= padded:
        if padded % candidate == 0:
            best = candidate
        candidate += 1
    return (padded // best, best)


def angle_table(rows_count, cols_count, period):
    phase = np.arange(rows_count)[:, None] * np.arange(cols_count)[None, :] % period
    phase = phase * (2.0 * math.pi / period)
    return (np.cos(phase), np.sin(phase))


def position_features(length, feat_count):
    freqs = np.array([3**j for j in range(feat_count // 2)])
    phase = (freqs[:, None] * np.arange(length)[None, :] % length) * (2.0 * math.pi / length)
    feats = np.stack([np.cos(phase), np.sin(phase)], axis=1).reshape(feat_count, length)
    return jnp.asarray(feats.astype(np.float32))


def bf16(table):
    return jnp.asarray(table.astype(np.float32)).astype(jnp.bfloat16)


def sizes(length):
    padded = 2 * length
    outer, inner = split_length(padded)
    half = outer // 2
    kept = half + 1
    held = -(-kept // 8) * 8
    return (padded, outer, inner, half, kept, held)


def packed_tables(length):
    padded, outer, inner, half, kept, held = sizes(length)
    b = np.arange(inner)[:, None, None]
    k = np.arange(held)[None, :, None]
    n = np.arange(half)[None, None, :]
    phase = (k * n * inner + k * b) % padded * (2.0 * math.pi / padded)
    live = (k < kept).astype(np.float64)
    first = np.stack([np.cos(phase) * live, -np.sin(phase) * live], axis=2)
    weight = live * np.where((k == 0) | (k == half), 1.0, 2.0) / padded
    last = np.stack([np.cos(phase) * weight, -np.sin(phase) * weight], axis=2)
    first = first.reshape(inner, 2 * held, half)
    last = last.reshape(inner, 2 * held, half).transpose(0, 2, 1)
    cb, sb = angle_table(inner, inner, inner)
    fwd = np.block([[cb, sb], [-sb, cb]])
    inv = np.block([[cb, -sb], [sb, cb]])
    return tuple(bf16(t) for t in (first, last, fwd, inv))


def dot32(a, b):
    return jnp.dot(a, b, preferred_element_type=jnp.float32)


def first_stage(dims, first_ref, pairs):
    _, _, inner, half, _, held = dims

    def body(b, carry):
        rows = [x[pl.ds(b, half, stride=inner), :].astype(jnp.bfloat16) for x, _ in pairs]
        out = dot32(first_ref[b], jnp.concatenate(rows, axis=1))
        for i, (_, s) in enumerate(pairs):
            s[pl.ds(b, 2 * held, stride=inner), :] = out[:, i * LANES : (i + 1) * LANES]
        return carry

    lax.fori_loop(0, inner, body, 0, unroll=4)


def last_stage(dims, last_ref, pairs):
    _, _, inner, half, _, held = dims

    def body(b, carry):
        rows = [s[pl.ds(b, 2 * held, stride=inner), :].astype(jnp.bfloat16) for s, _ in pairs]
        out = dot32(last_ref[b], jnp.concatenate(rows, axis=1))
        for i, (_, y) in enumerate(pairs):
            y[pl.ds(b, half, stride=inner), :] = out[:, i * LANES : (i + 1) * LANES]
        return carry

    lax.fori_loop(0, inner, body, 0, unroll=4)


def spectrum(dims, fwd_ref, t, after=None):
    _, _, inner, half, kept, held = dims

    def body(k, carry):
        at = pl.ds(pl.multiple_of(k * 2 * inner, 2 * inner), 2 * inner)
        spec = dot32(fwd_ref[...], t[at, :].astype(jnp.bfloat16))
        if after is None:
            t[at, :] = spec
        else:
            after(at, spec)
        return carry

    lax.fori_loop(0, kept, body, 0, unroll=5)


def slab_kernel(dims, count, q_ref, k_ref, v_ref, g_ref, h_ref, first_ref, last_ref, fwd_ref, inv_ref,
                gq_ref, gk_ref, gv_ref, df_ref,
                sent, held_rows, x, tu, th, td, tv, send_sem, recv_sem):
    _, _, inner, half, kept, held = dims
    me = lax.axis_index("seq")
    barrier = pltpu.get_barrier_semaphore()

    def peer(step):
        return lax.rem(me + step, count)

    def source(step):
        return lax.rem(me + count - step, count)

    def loop(body, start=1):
        def run(step, carry):
            body(step)
            return carry

        lax.fori_loop(start, count, run, 0)

    def lanes(j):
        return pl.ds(pl.multiple_of(j * LANES, LANES), LANES)

    tok = q_ref.shape[0]

    def rows(j):
        return pl.ds(pl.multiple_of(j * tok, tok), tok)

    def copy(array, step):
        return pltpu.make_async_remote_copy(
            src_ref=sent.at[array, peer(step)],
            dst_ref=held_rows.at[array, me],
            send_sem=send_sem.at[array, step],
            recv_sem=recv_sem.at[array, step],
            device_id={"seq": peer(step)},
            device_id_type=pl.DeviceIdType.MESH,
        )

    def send(array):
        loop(lambda step: copy(array, step).start())

    def receive(array):
        loop(lambda step: copy(array, step).wait_recv())

    def hold(array):
        held_rows[array, me] = sent[array, me]

    def gate(array, a, b):
        def body(j):
            sent[array, j] = product(a[:, lanes(j)], b[:, lanes(j)])

        loop(body, 0)

    def unpack(array):
        def body(j):
            x[rows(j), :] = held_rows[array, j].astype(jnp.float32)

        loop(body, 0)

    def pack(array):
        def body(j):
            sent[array, j] = x[rows(j), :].astype(jnp.bfloat16)

        loop(body, 0)

    loop(lambda step: pl.semaphore_signal(
        barrier, inc=1, device_id={"seq": peer(step)}, device_id_type=pl.DeviceIdType.MESH))
    gate(0, k_ref, v_ref)
    pl.semaphore_wait(barrier, count - 1)
    send(0)
    hold(0)
    gate(1, g_ref, q_ref)
    hold(1)
    tail = 2 * inner * (held - kept)
    tv[pl.ds(2 * inner * kept, tail), :] = jnp.zeros((tail, LANES), jnp.float32)
    x[...] = h_ref[...].astype(jnp.float32)
    first_stage(dims, first_ref, [(x, th)])
    spectrum(dims, fwd_ref, th)
    receive(0)
    send(1)
    unpack(0)
    first_stage(dims, first_ref, [(x, tu)])

    def convolve(at, su):
        tu[at, :] = su
        sh = th[at, :]
        ur, ui = su[:inner], su[inner:]
        hr, hi = sh[:inner], sh[inner:]
        prod = jnp.concatenate([hr * ur - hi * ui, hr * ui + hi * ur], axis=0)
        tv[at, :] = dot32(inv_ref[...], prod.astype(jnp.bfloat16))

    spectrum(dims, fwd_ref, tu, convolve)
    last_stage(dims, last_ref, [(tv, x)])
    pack(2)
    send(2)
    hold(2)
    receive(1)
    unpack(1)
    first_stage(dims, first_ref, [(x, td)])

    def correlate(at, sd):
        su, sh = tu[at, :], th[at, :]
        dr, di = sd[:inner], sd[inner:]
        ur, ui = su[:inner], su[inner:]
        hr, hi = sh[:inner], sh[inner:]
        real = jnp.concatenate([hr * dr + hi * di, ur * dr + ui * di], axis=1)
        imag = jnp.concatenate([hr * di - hi * dr, ur * di - ui * dr], axis=1)
        prod = jnp.concatenate([real, imag], axis=0).astype(jnp.bfloat16)
        out = dot32(inv_ref[...], prod)
        td[at, :] = out[:, :LANES]
        tv[at, :] = out[:, LANES:]

    spectrum(dims, fwd_ref, td, correlate)
    last_stage(dims, last_ref, [(td, x)])
    pack(3)
    send(3)
    hold(3)
    last_stage(dims, last_ref, [(tv, df_ref)])
    receive(2)

    def finish_q(j):
        gq_ref[:, lanes(j)] = product(g_ref[:, lanes(j)], held_rows[2, j])

    loop(finish_q, 0)
    receive(3)

    def finish_kv(j):
        du = held_rows[3, j]
        gk_ref[:, lanes(j)] = product(du, v_ref[:, lanes(j)])
        gv_ref[:, lanes(j)] = product(du, k_ref[:, lanes(j)])

    loop(finish_kv, 0)
    for array in range(4):
        loop(lambda step: copy(array, step).wait_send())


def packed_work(q, k, v, g, taps, count):
    length = taps.shape[0]
    tables = packed_tables(length)
    dims = sizes(length)
    _, _, inner, half, kept, held = dims
    row, full = (length, LANES), (2 * inner * held, LANES)
    blocks = (4, count, q.shape[0], LANES)
    gate = jax.ShapeDtypeStruct(q.shape, jnp.bfloat16)
    flops = 2 * LANES * 6 * (inner * 2 * held * half + kept * 4 * inner * inner)
    return pl.pallas_call(
        functools.partial(slab_kernel, dims, count),
        out_shape=[gate, gate, gate, jax.ShapeDtypeStruct(row, jnp.float32)],
        in_specs=[pl.BlockSpec(memory_space=pltpu.VMEM)] * 9,
        out_specs=[pl.BlockSpec(memory_space=pltpu.VMEM)] * 4,
        scratch_shapes=[
            pltpu.VMEM(blocks, jnp.bfloat16),
            pltpu.VMEM(blocks, jnp.bfloat16),
            pltpu.VMEM(row, jnp.float32),
            *[pltpu.VMEM(full, jnp.float32)] * 4,
            pltpu.SemaphoreType.DMA((4, count)),
            pltpu.SemaphoreType.DMA((4, count)),
        ],
        compiler_params=pltpu.CompilerParams(
            vmem_limit_bytes=60 * 2**20, collective_id=0, has_side_effects=True
        ),
        cost_estimate=pl.CostEstimate(flops=flops, bytes_accessed=2**24, transcendentals=0),
    )(q, k, v, g, taps, *tables)


def plain_tables(length):
    padded = 2 * length
    outer, inner = split_length(padded)
    oc, os = angle_table(outer, outer // 2, outer)
    tc, ts = angle_table(outer, inner, padded)
    ic, is_ = angle_table(inner, inner, inner)
    tc, ts = (jnp.asarray(t.astype(np.float32)) for t in (tc, ts))
    return (outer, inner, bf16(oc), bf16(os), tc, ts, bf16(ic), bf16(is_))


def forward_dft(signal, tables):
    outer, inner, outer_cos, outer_sin, twid_cos, twid_sin, inner_cos, inner_sin = tables
    blocks = signal.reshape(signal.shape[0], outer // 2, inner)
    part_re = jnp.einsum("kn,cnb->ckb", outer_cos, blocks, preferred_element_type=jnp.float32)
    part_im = -jnp.einsum("kn,cnb->ckb", outer_sin, blocks, preferred_element_type=jnp.float32)
    turn_re = (part_re * twid_cos + part_im * twid_sin).astype(jnp.bfloat16)
    turn_im = (part_im * twid_cos - part_re * twid_sin).astype(jnp.bfloat16)
    spec_re = jnp.einsum(
        "ckn,nm->ckm", turn_re, inner_cos, preferred_element_type=jnp.float32
    ) + jnp.einsum("ckn,nm->ckm", turn_im, inner_sin, preferred_element_type=jnp.float32)
    spec_im = jnp.einsum(
        "ckn,nm->ckm", turn_im, inner_cos, preferred_element_type=jnp.float32
    ) - jnp.einsum("ckn,nm->ckm", turn_re, inner_sin, preferred_element_type=jnp.float32)
    return (spec_re, spec_im)


def inverse_dft(spec_re, spec_im, tables):
    outer, inner, outer_cos, outer_sin, twid_cos, twid_sin, inner_cos, inner_sin = tables
    part_re = jnp.einsum(
        "ckm,mn->ckn", spec_re, inner_cos, preferred_element_type=jnp.float32
    ) - jnp.einsum("ckm,mn->ckn", spec_im, inner_sin, preferred_element_type=jnp.float32)
    part_im = jnp.einsum(
        "ckm,mn->ckn", spec_re, inner_sin, preferred_element_type=jnp.float32
    ) + jnp.einsum("ckm,mn->ckn", spec_im, inner_cos, preferred_element_type=jnp.float32)
    turn_re = (part_re * twid_cos - part_im * twid_sin).astype(jnp.bfloat16)
    turn_im = (part_re * twid_sin + part_im * twid_cos).astype(jnp.bfloat16)
    values = jnp.einsum(
        "kn,ckb->cnb", outer_cos, turn_re, preferred_element_type=jnp.float32
    ) - jnp.einsum("kn,ckb->cnb", outer_sin, turn_im, preferred_element_type=jnp.float32)
    return values.reshape(values.shape[0], outer // 2 * inner) / (outer * inner)


def spectral_products(first, second, conjugate):
    if conjugate:
        real_part = first[0] * second[0] + first[1] * second[1]
        imag_part = first[0] * second[1] - first[1] * second[0]
    else:
        real_part = first[0] * second[0] - first[1] * second[1]
        imag_part = first[0] * second[1] + first[1] * second[0]
    return (real_part.astype(jnp.bfloat16), imag_part.astype(jnp.bfloat16))


def plain_work(u, d, h, length):
    tables = plain_tables(length)
    spec_u = forward_dft(u.T, tables)
    spec_d = forward_dft(d.T, tables)
    spec_h = forward_dft(h.T, tables)
    z = inverse_dft(*spectral_products(spec_h, spec_u, False), tables)
    du = inverse_dft(*spectral_products(spec_h, spec_d, True), tables)
    df = inverse_dft(*spectral_products(spec_u, spec_d, True), tables)
    return (z.T.astype(jnp.bfloat16), du.T.astype(jnp.bfloat16), df.T)


def product(a, b):
    return (a.astype(jnp.float32) * b.astype(jnp.float32)).astype(jnp.bfloat16)


def to_channels(x, seq_count):
    tok, channels = x.shape
    x = x.reshape(tok, seq_count, channels // seq_count).transpose(1, 0, 2)
    x = lax.all_to_all(x, "seq", split_axis=0, concat_axis=0, tiled=True)
    return x.reshape(seq_count * tok, channels // seq_count)


def to_tokens(x, seq_count):
    length, width = x.shape
    x = x.reshape(seq_count, length // seq_count, width)
    x = lax.all_to_all(x, "seq", split_axis=0, concat_axis=0, tiled=True)
    return x.transpose(1, 0, 2).reshape(length // seq_count, seq_count * width)


def local(q_saved, k_saved, v_saved, grad_out, residue, rate, freq_mix):
    tok_dev, channels = q_saved.shape
    seq_count = lax.axis_size("seq")
    length = tok_dev * seq_count
    slab_width = channels // seq_count
    first_channel = lax.axis_index("ch") * channels + lax.axis_index("seq") * slab_width
    group_index = first_channel // (C // GROUPS)
    rate_row = lax.dynamic_slice_in_dim(rate, group_index, 1, 0)[0]
    mix_row = lax.dynamic_slice_in_dim(freq_mix, group_index, 1, 0)[0]
    times = jnp.arange(length, dtype=jnp.float32) / length
    feats = position_features(length, FEATS)
    pre = jnp.dot(mix_row, feats, precision=HIGH)
    window = jnp.exp(-rate_row[:, None] * times[None, :])
    basis = jnp.sin(pre) * window
    taps = lax.dot_general(
        basis, residue, (((0,), (1,)), ((), ())), precision=HIGH
    ).astype(jnp.bfloat16)
    if slab_width == LANES:
        grad_q, grad_k, grad_v, dfilter = packed_work(
            q_saved, k_saved, v_saved, grad_out, taps, seq_count
        )
    else:
        u = to_channels(product(k_saved, v_saved), seq_count)
        d = to_channels(product(grad_out, q_saved), seq_count)
        z, du, dfilter = plain_work(u, d, taps, length)
        z = to_tokens(z, seq_count)
        du = to_tokens(du, seq_count)
        grad_q = product(grad_out, z)
        grad_k = product(du, v_saved)
        grad_v = product(du, k_saved)
    grad_residue = lax.dot_general(
        dfilter, basis, (((0,), (1,)), ((), ())), precision=HIGH
    ) / length
    mixed = lax.dot_general(residue, dfilter, (((0,), (1,)), ((), ())), precision=HIGH)
    rate_part = -jnp.sum(mixed * times[None, :] * basis, axis=1) / length
    slope = mixed * window * jnp.cos(pre)
    mix_part = jnp.dot(slope, feats.T, precision=HIGH) / length
    selector = (jnp.arange(GROUPS, dtype=jnp.int32) == group_index).astype(jnp.float32)
    rate_total = selector[:, None] * rate_part[None, :]
    mix_total = selector[:, None, None] * mix_part[None, :, :]
    grad_rate, grad_mix = lax.psum((rate_total, mix_total), ("seq", "ch"))
    return (grad_q, grad_k, grad_v, grad_residue, grad_rate, grad_mix)


def solution(mesh):
    return jax.shard_map(
        local,
        mesh=mesh,
        in_specs=(
            P("seq", "ch"),
            P("seq", "ch"),
            P("seq", "ch"),
            P("seq", "ch"),
            P(("ch", "seq"), None),
            P(),
            P(),
        ),
        out_specs=(
            P("seq", "ch"),
            P("seq", "ch"),
            P("seq", "ch"),
            P(("ch", "seq"), None),
            P(),
            P(),
        ),
        check_vma=False,
    )
```

```python
import functools
import math

import jax
import jax.numpy as jnp
import numpy as np
from jax import lax
from jax.experimental import pallas as pl
from jax.experimental.pallas import tpu as pltpu
from jax.sharding import PartitionSpec as P

C = 4096
FEATS = 16
GROUPS = 4
LANES = 128


HIGH = lax.Precision.HIGHEST


def split_length(padded):
    best = 1
    candidate = 1
    while candidate * candidate <= padded:
        if padded % candidate == 0:
            best = candidate
        candidate += 1
    return (padded // best, best)


def angle_table(rows_count, cols_count, period):
    phase = np.arange(rows_count)[:, None] * np.arange(cols_count)[None, :] % period
    phase = phase * (2.0 * math.pi / period)
    return (np.cos(phase), np.sin(phase))


def position_features(length, feat_count):
    freqs = np.array([3**j for j in range(feat_count // 2)])
    phase = (freqs[:, None] * np.arange(length)[None, :] % length) * (2.0 * math.pi / length)
    feats = np.stack([np.cos(phase), np.sin(phase)], axis=1).reshape(feat_count, length)
    return jnp.asarray(feats.astype(np.float32))


def bf16(table):
    return jnp.asarray(table.astype(np.float32)).astype(jnp.bfloat16)


def sizes(length):
    padded = 2 * length
    outer, inner = split_length(padded)
    half = outer // 2
    kept = half + 1
    held = -(-kept // 8) * 8
    return (padded, outer, inner, half, kept, held)


def packed_tables(length):
    padded, outer, inner, half, kept, held = sizes(length)
    b = np.arange(inner)[:, None, None]
    k = np.arange(held)[None, :, None]
    n = np.arange(half)[None, None, :]
    phase = (k * n * inner + k * b) % padded * (2.0 * math.pi / padded)
    live = (k < kept).astype(np.float64)
    first = np.stack([np.cos(phase) * live, -np.sin(phase) * live], axis=2)
    weight = live * np.where((k == 0) | (k == half), 1.0, 2.0) / padded
    last = np.stack([np.cos(phase) * weight, -np.sin(phase) * weight], axis=2)
    first = first.reshape(inner, 2 * held, half)
    last = last.reshape(inner, 2 * held, half).transpose(0, 2, 1)
    cb, sb = angle_table(inner, inner, inner)
    fwd = np.block([[cb, sb], [-sb, cb]])
    inv = np.block([[cb, -sb], [sb, cb]])
    return tuple(bf16(t) for t in (first, last, fwd, inv))


def dot32(a, b):
    return jnp.dot(a, b, preferred_element_type=jnp.float32)


def first_stage(dims, first_ref, pairs):
    _, _, inner, half, _, held = dims

    def body(b, carry):
        rows = [x[pl.ds(b, half, stride=inner), :].astype(jnp.bfloat16) for x, _ in pairs]
        out = dot32(first_ref[b], jnp.concatenate(rows, axis=1))
        for i, (_, s) in enumerate(pairs):
            s[pl.ds(b, 2 * held, stride=inner), :] = out[:, i * LANES : (i + 1) * LANES]
        return carry

    lax.fori_loop(0, inner, body, 0, unroll=4)


def last_stage(dims, last_ref, pairs):
    _, _, inner, half, _, held = dims

    def body(b, carry):
        rows = [s[pl.ds(b, 2 * held, stride=inner), :].astype(jnp.bfloat16) for s, _ in pairs]
        out = dot32(last_ref[b], jnp.concatenate(rows, axis=1))
        for i, (_, y) in enumerate(pairs):
            y[pl.ds(b, half, stride=inner), :] = out[:, i * LANES : (i + 1) * LANES]
        return carry

    lax.fori_loop(0, inner, body, 0, unroll=4)


def spectrum(dims, fwd_ref, t, after=None):
    _, _, inner, half, kept, held = dims

    def body(k, carry):
        at = pl.ds(pl.multiple_of(k * 2 * inner, 2 * inner), 2 * inner)
        spec = dot32(fwd_ref[...], t[at, :].astype(jnp.bfloat16))
        if after is None:
            t[at, :] = spec
        else:
            after(at, spec)
        return carry

    lax.fori_loop(0, kept, body, 0, unroll=5)


def sin_cos(angle):
    turns = jnp.round(angle * (2.0 / math.pi))
    r = angle - turns * 1.5703125
    r = r - turns * 4.837512969970703e-4
    r = r - turns * 7.549789954891882e-8
    z = r * r
    s = r + r * z * (-1.6666654611e-1 + z * (8.3321608736e-3 - z * 1.9515295891e-4))
    c = 1.0 - 0.5 * z + z * z * (
        4.166664568298827e-2 + z * (-1.388731625493765e-3 + z * 2.443315711809948e-5)
    )

    def parity(value):
        return value - 2.0 * jnp.floor(value * 0.5)

    odd = parity(turns)
    even = 1.0 - odd
    sin_sign = 1.0 - 2.0 * parity(jnp.floor(turns * 0.5))
    cos_sign = 1.0 - 2.0 * parity(jnp.floor((turns + 1.0) * 0.5))
    return (sin_sign * (even * s + odd * c), cos_sign * (even * c + odd * s))


def dot_high(a, b, dims):
    return lax.dot_general(
        a, b, (dims, ((), ())), precision=HIGH, preferred_element_type=jnp.float32
    )


def slab_kernel(dims, count, slabs, q_ref, k_ref, v_ref, g_ref, res_ref, rate_ref, mix_ref, feats_ref,
                first_ref, last_ref, fwd_ref, inv_ref,
                gq_ref, gk_ref, gv_ref, gres_ref, small_ref,
                sent, held_rows, x, tu, th, td, tv, basis, slope, part, parts, sums, allsums,
                send_sem, recv_sem, part_send, part_recv, sum_send, sum_recv):
    _, _, inner, half, kept, held = dims
    length = x.shape[0]
    col = lax.axis_index("ch")
    per_group = C // GROUPS // LANES
    me = lax.axis_index("seq")
    barrier = pltpu.get_barrier_semaphore()

    def peer(step):
        return lax.rem(me + step, count)

    def source(step):
        return lax.rem(me + count - step, count)

    def loop(body, start=1):
        def run(step, carry):
            body(step)
            return carry

        lax.fori_loop(start, count, run, 0)

    def lanes(j):
        return pl.ds(pl.multiple_of(j * LANES, LANES), LANES)

    tok = q_ref.shape[0]

    def rows(j):
        return pl.ds(pl.multiple_of(j * tok, tok), tok)

    def copy(array, step):
        return pltpu.make_async_remote_copy(
            src_ref=sent.at[array, peer(step)],
            dst_ref=held_rows.at[array, me],
            send_sem=send_sem.at[array, step],
            recv_sem=recv_sem.at[array, step],
            device_id={"seq": peer(step)},
            device_id_type=pl.DeviceIdType.MESH,
        )

    def send(array):
        loop(lambda step: copy(array, step).start())

    def receive(array):
        loop(lambda step: copy(array, step).wait_recv())

    def hold(array):
        held_rows[array, me] = sent[array, me]

    def gate(array, a, b):
        def body(j):
            sent[array, j] = product(a[:, lanes(j)], b[:, lanes(j)])

        loop(body, 0)

    def unpack(array):
        def body(j):
            x[rows(j), :] = held_rows[array, j].astype(jnp.float32)

        loop(body, 0)

    def pack(array):
        def body(j):
            sent[array, j] = x[rows(j), :].astype(jnp.bfloat16)

        loop(body, 0)

    def part_copy(step):
        return pltpu.make_async_remote_copy(
            src_ref=part,
            dst_ref=parts.at[me],
            send_sem=part_send.at[step],
            recv_sem=part_recv.at[step],
            device_id={"seq": peer(step)},
            device_id_type=pl.DeviceIdType.MESH,
        )

    def sum_copy(step):
        return pltpu.make_async_remote_copy(
            src_ref=sums,
            dst_ref=allsums.at[col],
            send_sem=sum_send.at[step],
            recv_sem=sum_recv.at[step],
            device_id={"ch": lax.rem(col + step, slabs)},
            device_id_type=pl.DeviceIdType.MESH,
        )

    def time(shape, j):
        steps = lax.broadcasted_iota(jnp.int32, shape, 1) + j * tok
        return steps.astype(jnp.float32) / length

    def taps(j):
        at = pl.ds(pl.multiple_of(j * tok, tok), tok)
        pre = dot_high(mix_ref[...], feats_ref[:, at], ((1,), (0,)))
        window = jnp.exp(-rate_ref[...] * time(pre.shape, j))
        sin, cos = sin_cos(pre)
        basis[:, at] = sin * window
        slope[:, at] = cos * window
        filt = dot_high(sin * window, res_ref[...], ((0,), (0,)))
        x[at, :] = filt.astype(jnp.bfloat16).astype(jnp.float32)

    def reduce(j, carry):
        gres, mix, rate = carry
        at = pl.ds(pl.multiple_of(j * tok, tok), tok)
        df = x[at, :]
        base = basis[:, at]
        mixed = dot_high(res_ref[...], df, ((1,), (1,)))
        gres = gres + dot_high(base, df, ((1,), (0,)))
        mix = mix + dot_high(feats_ref[:, at], mixed * slope[:, at], ((1,), (1,)))
        rate = rate + dot_high(time((8, tok), j), mixed * base, ((1,), (1,)))
        return (gres, mix, rate)

    loop(lambda step: pl.semaphore_signal(
        barrier, inc=1, device_id={"seq": peer(step)}, device_id_type=pl.DeviceIdType.MESH))
    for step in range(1, slabs):
        pl.semaphore_signal(barrier, inc=1, device_id={"ch": lax.rem(col + step, slabs)},
                            device_id_type=pl.DeviceIdType.MESH)
    gate(0, k_ref, v_ref)
    pl.semaphore_wait(barrier, count + slabs - 2)
    send(0)
    hold(0)
    gate(1, g_ref, q_ref)
    hold(1)
    tail = 2 * inner * (held - kept)
    tv[pl.ds(2 * inner * kept, tail), :] = jnp.zeros((tail, LANES), jnp.float32)
    loop(taps, 0)
    first_stage(dims, first_ref, [(x, th)])
    spectrum(dims, fwd_ref, th)
    receive(0)
    send(1)
    unpack(0)
    first_stage(dims, first_ref, [(x, tu)])

    def convolve(at, su):
        tu[at, :] = su
        sh = th[at, :]
        ur, ui = su[:inner], su[inner:]
        hr, hi = sh[:inner], sh[inner:]
        prod = jnp.concatenate([hr * ur - hi * ui, hr * ui + hi * ur], axis=0)
        tv[at, :] = dot32(inv_ref[...], prod.astype(jnp.bfloat16))

    spectrum(dims, fwd_ref, tu, convolve)
    last_stage(dims, last_ref, [(tv, x)])
    pack(2)
    send(2)
    hold(2)
    receive(1)
    unpack(1)
    first_stage(dims, first_ref, [(x, td)])

    def correlate(at, sd):
        su, sh = tu[at, :], th[at, :]
        dr, di = sd[:inner], sd[inner:]
        ur, ui = su[:inner], su[inner:]
        hr, hi = sh[:inner], sh[inner:]
        real = jnp.concatenate([hr * dr + hi * di, ur * dr + ui * di], axis=1)
        imag = jnp.concatenate([hr * di - hi * dr, ur * di - ui * dr], axis=1)
        prod = jnp.concatenate([real, imag], axis=0).astype(jnp.bfloat16)
        out = dot32(inv_ref[...], prod)
        td[at, :] = out[:, :LANES]
        tv[at, :] = out[:, LANES:]

    spectrum(dims, fwd_ref, td, correlate)
    last_stage(dims, last_ref, [(td, x)])
    pack(3)
    send(3)
    hold(3)
    last_stage(dims, last_ref, [(tv, x)])
    modes, feats = mix_ref.shape
    zeros = [jnp.zeros(shape, jnp.float32) for shape in ((modes, LANES), (feats, modes), (8, modes))]
    gres, mix, rate = lax.fori_loop(0, count, reduce, tuple(zeros))
    gres_ref[...] = gres / length
    part[...] = jnp.zeros_like(part)
    part[:feats, :modes] = mix / length
    part[feats:, :modes] = -rate / length
    loop(lambda step: part_copy(step).start())
    parts[me] = part[...]
    receive(2)

    def finish_q(j):
        gq_ref[:, lanes(j)] = product(g_ref[:, lanes(j)], held_rows[2, j])

    loop(finish_q, 0)
    loop(lambda step: part_copy(step).wait_recv())
    for group in range(count // per_group):
        total = parts[group * per_group]
        for j in range(1, per_group):
            total = total + parts[group * per_group + j]
        sums[group] = total
    for step in range(1, slabs):
        sum_copy(step).start()
    allsums[col] = sums[...]
    receive(3)

    def finish_kv(j):
        du = held_rows[3, j]
        gk_ref[:, lanes(j)] = product(du, v_ref[:, lanes(j)])
        gv_ref[:, lanes(j)] = product(du, k_ref[:, lanes(j)])

    loop(finish_kv, 0)
    for step in range(1, slabs):
        sum_copy(step).wait_recv()
    small_ref[...] = allsums[...]
    for array in range(4):
        loop(lambda step: copy(array, step).wait_send())
    loop(lambda step: part_copy(step).wait_send())
    for step in range(1, slabs):
        sum_copy(step).wait_send()


def packed_work(q, k, v, g, residue, rate_row, mix_row, feats, count, slabs):
    length = feats.shape[1]
    modes = mix_row.shape[0]
    tables = packed_tables(length)
    dims = sizes(length)
    _, _, inner, half, kept, held = dims
    row, full = (length, LANES), (2 * inner * held, LANES)
    blocks = (4, count, q.shape[0], LANES)
    gate = jax.ShapeDtypeStruct(q.shape, jnp.bfloat16)
    part = (FEATS + 8, LANES)
    sums = (count * LANES // (C // GROUPS), *part)
    flops = 2 * LANES * 6 * (inner * 2 * held * half + kept * 4 * inner * inner)
    args = (q, k, v, g, residue.T, rate_row[:, None], mix_row, feats, *tables)
    f32 = functools.partial(jax.ShapeDtypeStruct, dtype=jnp.float32)
    grad_q, grad_k, grad_v, gres, small = pl.pallas_call(
        functools.partial(slab_kernel, dims, count, slabs),
        out_shape=[gate, gate, gate, f32((modes, LANES)), f32((slabs, *sums))],
        in_specs=[pl.BlockSpec(memory_space=pltpu.VMEM)] * len(args),
        out_specs=[pl.BlockSpec(memory_space=pltpu.VMEM)] * 5,
        scratch_shapes=[
            pltpu.VMEM(blocks, jnp.bfloat16),
            pltpu.VMEM(blocks, jnp.bfloat16),
            pltpu.VMEM(row, jnp.float32),
            *[pltpu.VMEM(full, jnp.float32)] * 4,
            *[pltpu.VMEM((modes, length), jnp.float32)] * 2,
            pltpu.VMEM(part, jnp.float32),
            pltpu.VMEM((count, *part), jnp.float32),
            pltpu.VMEM(sums, jnp.float32),
            pltpu.VMEM((slabs, *sums), jnp.float32),
            pltpu.SemaphoreType.DMA((4, count)),
            pltpu.SemaphoreType.DMA((4, count)),
            *[pltpu.SemaphoreType.DMA((count,))] * 2,
            *[pltpu.SemaphoreType.DMA((slabs,))] * 2,
        ],
        compiler_params=pltpu.CompilerParams(
            vmem_limit_bytes=60 * 2**20, collective_id=0, has_side_effects=True
        ),
        cost_estimate=pl.CostEstimate(flops=flops, bytes_accessed=2**24, transcendentals=0),
    )(*args)
    small = small.reshape(GROUPS, *part)
    grad_mix = small[:, :FEATS, :modes].transpose(0, 2, 1)
    return (grad_q, grad_k, grad_v, gres.T, small[:, FEATS, :modes], grad_mix)


def plain_tables(length):
    padded = 2 * length
    outer, inner = split_length(padded)
    oc, os = angle_table(outer, outer // 2, outer)
    tc, ts = angle_table(outer, inner, padded)
    ic, is_ = angle_table(inner, inner, inner)
    tc, ts = (jnp.asarray(t.astype(np.float32)) for t in (tc, ts))
    return (outer, inner, bf16(oc), bf16(os), tc, ts, bf16(ic), bf16(is_))


def forward_dft(signal, tables):
    outer, inner, outer_cos, outer_sin, twid_cos, twid_sin, inner_cos, inner_sin = tables
    blocks = signal.reshape(signal.shape[0], outer // 2, inner)
    part_re = jnp.einsum("kn,cnb->ckb", outer_cos, blocks, preferred_element_type=jnp.float32)
    part_im = -jnp.einsum("kn,cnb->ckb", outer_sin, blocks, preferred_element_type=jnp.float32)
    turn_re = (part_re * twid_cos + part_im * twid_sin).astype(jnp.bfloat16)
    turn_im = (part_im * twid_cos - part_re * twid_sin).astype(jnp.bfloat16)
    spec_re = jnp.einsum(
        "ckn,nm->ckm", turn_re, inner_cos, preferred_element_type=jnp.float32
    ) + jnp.einsum("ckn,nm->ckm", turn_im, inner_sin, preferred_element_type=jnp.float32)
    spec_im = jnp.einsum(
        "ckn,nm->ckm", turn_im, inner_cos, preferred_element_type=jnp.float32
    ) - jnp.einsum("ckn,nm->ckm", turn_re, inner_sin, preferred_element_type=jnp.float32)
    return (spec_re, spec_im)


def inverse_dft(spec_re, spec_im, tables):
    outer, inner, outer_cos, outer_sin, twid_cos, twid_sin, inner_cos, inner_sin = tables
    part_re = jnp.einsum(
        "ckm,mn->ckn", spec_re, inner_cos, preferred_element_type=jnp.float32
    ) - jnp.einsum("ckm,mn->ckn", spec_im, inner_sin, preferred_element_type=jnp.float32)
    part_im = jnp.einsum(
        "ckm,mn->ckn", spec_re, inner_sin, preferred_element_type=jnp.float32
    ) + jnp.einsum("ckm,mn->ckn", spec_im, inner_cos, preferred_element_type=jnp.float32)
    turn_re = (part_re * twid_cos - part_im * twid_sin).astype(jnp.bfloat16)
    turn_im = (part_re * twid_sin + part_im * twid_cos).astype(jnp.bfloat16)
    values = jnp.einsum(
        "kn,ckb->cnb", outer_cos, turn_re, preferred_element_type=jnp.float32
    ) - jnp.einsum("kn,ckb->cnb", outer_sin, turn_im, preferred_element_type=jnp.float32)
    return values.reshape(values.shape[0], outer // 2 * inner) / (outer * inner)


def spectral_products(first, second, conjugate):
    if conjugate:
        real_part = first[0] * second[0] + first[1] * second[1]
        imag_part = first[0] * second[1] - first[1] * second[0]
    else:
        real_part = first[0] * second[0] - first[1] * second[1]
        imag_part = first[0] * second[1] + first[1] * second[0]
    return (real_part.astype(jnp.bfloat16), imag_part.astype(jnp.bfloat16))


def plain_work(u, d, h, length):
    tables = plain_tables(length)
    spec_u = forward_dft(u.T, tables)
    spec_d = forward_dft(d.T, tables)
    spec_h = forward_dft(h.T, tables)
    z = inverse_dft(*spectral_products(spec_h, spec_u, False), tables)
    du = inverse_dft(*spectral_products(spec_h, spec_d, True), tables)
    df = inverse_dft(*spectral_products(spec_u, spec_d, True), tables)
    return (z.T.astype(jnp.bfloat16), du.T.astype(jnp.bfloat16), df.T)


def product(a, b):
    return (a.astype(jnp.float32) * b.astype(jnp.float32)).astype(jnp.bfloat16)


def to_channels(x, seq_count):
    tok, channels = x.shape
    x = x.reshape(tok, seq_count, channels // seq_count).transpose(1, 0, 2)
    x = lax.all_to_all(x, "seq", split_axis=0, concat_axis=0, tiled=True)
    return x.reshape(seq_count * tok, channels // seq_count)


def to_tokens(x, seq_count):
    length, width = x.shape
    x = x.reshape(seq_count, length // seq_count, width)
    x = lax.all_to_all(x, "seq", split_axis=0, concat_axis=0, tiled=True)
    return x.transpose(1, 0, 2).reshape(length // seq_count, seq_count * width)


def local(q_saved, k_saved, v_saved, grad_out, residue, rate, freq_mix):
    tok_dev, channels = q_saved.shape
    seq_count = lax.axis_size("seq")
    length = tok_dev * seq_count
    slab_width = channels // seq_count
    first_channel = lax.axis_index("ch") * channels + lax.axis_index("seq") * slab_width
    group_index = first_channel // (C // GROUPS)
    rate_row = lax.dynamic_slice_in_dim(rate, group_index, 1, 0)[0]
    mix_row = lax.dynamic_slice_in_dim(freq_mix, group_index, 1, 0)[0]
    feats = position_features(length, FEATS)
    slabs = lax.axis_size("ch")
    if slab_width == LANES and slabs * channels == C and channels % (C // GROUPS) == 0:
        return packed_work(
            q_saved, k_saved, v_saved, grad_out, residue, rate_row, mix_row, feats, seq_count, slabs
        )
    times = jnp.arange(length, dtype=jnp.float32) / length
    pre = jnp.dot(mix_row, feats, precision=HIGH)
    window = jnp.exp(-rate_row[:, None] * times[None, :])
    basis = jnp.sin(pre) * window
    taps = lax.dot_general(
        basis, residue, (((0,), (1,)), ((), ())), precision=HIGH
    ).astype(jnp.bfloat16)
    u = to_channels(product(k_saved, v_saved), seq_count)
    d = to_channels(product(grad_out, q_saved), seq_count)
    z, du, dfilter = plain_work(u, d, taps, length)
    z = to_tokens(z, seq_count)
    du = to_tokens(du, seq_count)
    grad_q = product(grad_out, z)
    grad_k = product(du, v_saved)
    grad_v = product(du, k_saved)
    grad_residue = lax.dot_general(
        dfilter, basis, (((0,), (1,)), ((), ())), precision=HIGH
    ) / length
    mixed = lax.dot_general(residue, dfilter, (((0,), (1,)), ((), ())), precision=HIGH)
    rate_part = -jnp.sum(mixed * times[None, :] * basis, axis=1) / length
    slope = mixed * window * jnp.cos(pre)
    mix_part = jnp.dot(slope, feats.T, precision=HIGH) / length
    selector = (jnp.arange(GROUPS, dtype=jnp.int32) == group_index).astype(jnp.float32)
    rate_total = selector[:, None] * rate_part[None, :]
    mix_total = selector[:, None, None] * mix_part[None, :, :]
    grad_rate, grad_mix = lax.psum((rate_total, mix_total), ("seq", "ch"))
    return (grad_q, grad_k, grad_v, grad_residue, grad_rate, grad_mix)


def solution(mesh):
    return jax.shard_map(
        local,
        mesh=mesh,
        in_specs=(
            P("seq", "ch"),
            P("seq", "ch"),
            P("seq", "ch"),
            P("seq", "ch"),
            P(("ch", "seq"), None),
            P(),
            P(),
        ),
        out_specs=(
            P("seq", "ch"),
            P("seq", "ch"),
            P("seq", "ch"),
            P(("ch", "seq"), None),
            P(),
            P(),
        ),
        check_vma=False,
    )
```
